32 devices in a mesh: dp: 4 (over y, x), seq: 8 (over z, core).
Axes of the slice: x: 2, y: 2, z: 4, core: 2. Of those that a mesh axis runs over, the one named last changes fastest.
Arguments:
- tokens: bfloat16 [32768, 1152], P(('dp', 'seq')), parts along dimension 0, may hold values from -6 to 6
- norm_gain: float32 [1152], replicated, may hold values from 0.4 to 2.5
- norm_bias: float32 [1152], replicated, may hold values from -3 to 3
- qkv_weight: bfloat16 [1152, 1728], replicated, may hold values from -1.5 to 1.5, as said below
- out_weight: bfloat16 [576, 1152], replicated, may hold values from -0.25 to 0.25
- segment_ids: int32 [32768], P(('dp', 'seq')), parts along dimension 0, may hold values from 0 to 8191, as said below
- dest_map: int32 [32768], P(('dp', 'seq')), parts along dimension 0, may hold values from 0 to 8191, as said below
Outputs:
- language: bfloat16 [32768, 1152], P(('dp', 'seq')), parts along dimension 0
The draws below stay inside these ranges and needn't reach their ends.
There are 4 independent parts, one for each index of `dp`. The reference program is written for one: setup_inputs(seed, part) draws one part's arguments, and reference() takes and returns one part's arrays. A program takes and returns all parts, laid end to end along the dimension named above; an argument that names none is the same for every part. Nothing has to cross between parts.
Inputs may be any that keep to these rules, and one draw needn't show every extreme that they name: `segment_ids`: ids never fall along the tokens; an image's tokens lie within one run of 1024 tokens, and within a run each new image takes the next id. In some run all tokens form one image. `dest_map`: A permutation. The tokens of one run go to exactly 4 runs of the language layout (row // 1024), exactly 256 tokens to each. `qkv_weight`: the three groups of columns are the query, key and value projections.
All inputs are finite; a program needn't handle non-finite values.
Results may differ from the reference program's by a relative error of at most 0.0057.
Values may be sent and summed in bfloat16 or wider, within the bound.
A program may use at most 128 MiB of HBM per device.

```python
import math
import jax
import jax.numpy as jnp
from jax import lax

D = 1152
HEADS = 8
HEAD_DIM = 72
BLOCK = 128
TOK_DEV = 1024
TOKENS = 8192
N_SEQ = 8


def draw_qkv_weight(key, part):
    width = HEADS * HEAD_DIM
    first, second, third = jax.random.split(jax.random.fold_in(key, 5), 3)
    queries = jax.random.normal(first, (D, width), jnp.float32) * D ** (-0.5)
    values = jax.random.normal(third, (D, width), jnp.float32) * D ** (-0.5)
    noise = jax.random.normal(second, (D, width), jnp.float32) * D ** (-0.5)
    keyed = noise
    joined = jnp.concatenate([queries, keyed, values], axis=1)
    return jnp.clip(joined, -1.5, 1.5).astype(jnp.bfloat16)


def draw_segment_ids(key, part):
    count_key, pick_key, order_key = jax.random.split(jax.random.fold_in(key, 11), 3)
    block_count = TOK_DEV // BLOCK
    cuts = jax.random.randint(count_key, (N_SEQ, 1), 0, 8 * block_count)
    picked = jax.random.randint(pick_key, (), 0, N_SEQ)
    cuts = jnp.where(jnp.arange(N_SEQ)[:, None] == picked, 0, cuts)
    ranks = jax.vmap(lambda single: jax.random.permutation(single, TOK_DEV))(jax.random.split(order_key, N_SEQ))
    starts = (ranks < cuts) & (jnp.arange(TOK_DEV)[None, :] > 0)
    local = jnp.cumsum(starts.astype(jnp.int32), axis=1)
    ids = jnp.arange(N_SEQ)[:, None] * TOK_DEV + local
    return ids.reshape(-1).astype(jnp.int32)


def draw_dest_map(key, part):
    groups = N_SEQ // 2
    capacity = TOK_DEV * 2 // N_SEQ
    offset_key, order_key = jax.random.split(jax.random.fold_in(key, 23))
    offsets = jax.random.permutation(offset_key, N_SEQ)[:groups]
    ranks = jax.vmap(lambda single: jax.random.permutation(single, TOK_DEV))(jax.random.split(order_key, N_SEQ))
    group = ranks // capacity
    within = ranks % capacity
    source = jnp.arange(N_SEQ)[:, None]
    target = (source + offsets[group]) % N_SEQ
    position = group * capacity + within
    return (target * TOK_DEV + position).reshape(-1).astype(jnp.int32)


def shard_levels(rng, extent, pieces, low, top_value):
    def one(axis_at, shards_of):
        heights = jax.random.uniform(jax.random.fold_in(jax.random.fold_in(rng, 6), axis_at), (shards_of,), jnp.float32, low / len(pieces), top_value / len(pieces))
        return jnp.repeat(jnp.exp(heights), extent[axis_at] // shards_of).reshape((-1,) + (1,) * (len(extent) - axis_at - 1))

    factor_of = one(*pieces[0])
    for cut in pieces[1:]:
        factor_of = factor_of * one(*cut)
    return factor_of


def normal_values(stream_key, dims, scale, most, cuts=(), kind=jnp.bfloat16):
    values = scale * jax.random.normal(stream_key, dims, jnp.float32)
    if cuts:
        values = values * shard_levels(stream_key, dims, cuts, -0.22, 0.18)
    return jnp.clip(values, -most, most).astype(kind)


def setup_inputs(seed: int = 0, part: int = 0) -> dict:
    streams_of = jax.random.split(jax.random.key(seed), 8)
    part_keys = jax.random.split(jax.random.fold_in(streams_of[7], part), 8)
    return {
        "tokens": normal_values(part_keys[0], (TOKENS, D), 1.0, 6.0, ((0, 8),)),
        "norm_gain": jnp.clip(jnp.exp(jax.random.uniform(streams_of[1], (D,), jnp.float32, math.log(0.4), math.log(2.5))), 0.4, 2.5),
        "norm_bias": normal_values(streams_of[2], (D,), 0.5, 3.0, (), jnp.float32),
        "qkv_weight": draw_qkv_weight(jax.random.fold_in(streams_of[7], 71), part),
        "out_weight": normal_values(streams_of[4], (HEADS * HEAD_DIM, D), (HEADS * HEAD_DIM) ** -0.5, 0.25),
        "segment_ids": draw_segment_ids(jax.random.fold_in(jax.random.fold_in(streams_of[7], part), 71), part),
        "dest_map": draw_dest_map(jax.random.fold_in(jax.random.fold_in(streams_of[7], part), 71), part),
    }


masked_fill = -1e+30

def normalize(row_block, norm_gain, norm_bias):
    values = row_block.astype(jnp.float32)
    center = values - lax.optimization_barrier(jnp.mean(values, axis=1, keepdims=True))
    spread = lax.optimization_barrier(jnp.mean(center * center, axis=1, keepdims=True))
    scaled = center * lax.rsqrt(spread + 1e-06) * norm_gain + norm_bias
    return scaled.astype(jnp.bfloat16)

def pair_partial(queries, key_block, value_block, query_ids, key_ids):
    scores = jnp.einsum('hdq,hdk->hqk', queries.astype(jnp.float32), key_block.astype(jnp.float32)) * HEAD_DIM ** (-0.5)
    allowed = (query_ids[:, None] == key_ids[None, :])[None]
    masked = jnp.where(allowed, scores, masked_fill)
    maxima = lax.optimization_barrier(jnp.max(masked, axis=2))
    weights = jnp.where(allowed, jnp.exp(masked - maxima[:, :, None]), 0.0)
    totals = lax.optimization_barrier(jnp.sum(weights, axis=2))
    rounded = weights.astype(jnp.bfloat16).astype(jnp.float32)
    summed = jnp.einsum('hqk,hdk->hdq', rounded, value_block.astype(jnp.float32))
    return (maxima, totals, summed)

def reference(tokens, norm_gain, norm_bias, qkv_weight, out_weight, segment_ids, dest_map):
    block_count = TOK_DEV // BLOCK
    pair_count = block_count * block_count
    pair_query = (jnp.arange(pair_count) // block_count).astype(jnp.int32)
    pair_keys = (jnp.arange(pair_count) % block_count).astype(jnp.int32)
    weight_heads = out_weight.reshape(HEADS, HEAD_DIM, D).astype(jnp.float32)

    def one_run(inputs):
        row_block, run_ids = inputs
        normed = normalize(row_block, norm_gain, norm_bias)
        projected = jnp.dot(normed, qkv_weight, preferred_element_type=jnp.float32).astype(jnp.bfloat16)
        blocks = projected.reshape(block_count, BLOCK, 3, HEADS, HEAD_DIM).transpose(0, 2, 3, 4, 1)
        id_blocks = run_ids.reshape(block_count, BLOCK)

        def one_pair(pair_index):
            q_block = pair_query[pair_index]
            k_block = pair_keys[pair_index]
            return pair_partial(blocks[q_block, 0], blocks[k_block, 1], blocks[k_block, 2], id_blocks[q_block], id_blocks[k_block])
        maxima, totals, summed = lax.map(one_pair, jnp.arange(pair_count, dtype=jnp.int32))
        maxima = maxima.reshape(block_count, block_count, HEADS, BLOCK)
        totals = totals.reshape(block_count, block_count, HEADS, BLOCK)
        summed = summed.reshape(block_count, block_count, HEADS, HEAD_DIM, BLOCK)
        highest = lax.optimization_barrier(jnp.max(maxima, axis=1))
        scales = jnp.exp(maxima - highest[:, None])
        denom = lax.optimization_barrier(jnp.sum(scales * totals, axis=1))
        numer = lax.optimization_barrier(jnp.sum(scales[:, :, :, None, :] * summed, axis=1))
        attended = (numer / denom[:, :, None, :]).astype(jnp.bfloat16)
        mixed = jnp.einsum('nhdb,hde->nbe', attended.astype(jnp.float32), weight_heads).reshape(TOK_DEV, D)
        return (row_block.astype(jnp.float32) + mixed).astype(jnp.bfloat16)
    vision = lax.map(one_run, (tokens.reshape(N_SEQ, TOK_DEV, D), segment_ids.reshape(N_SEQ, TOK_DEV)))
    vision = vision.reshape(TOKENS, D)
    return jnp.zeros_like(vision).at[dest_map].set(vision)
```

```python
import functools
import math

import jax
import jax.numpy as jnp
from jax import lax
from jax.experimental import pallas as pl
from jax.experimental.pallas import tpu as pltpu
from jax.sharding import PartitionSpec as P

HEADS = 8
HEAD_DIM = 72
LANES = 128
ROWS = 256
VMEM = pl.BlockSpec(memory_space=pltpu.VMEM)
masked_fill = -1e30


def route_kernel(count, cap, rel_ref, pos_ref, slot_ref, place_ref):
    run = rel_ref.shape[1]
    rel = rel_ref[...]
    shifts = lax.broadcasted_iota(jnp.int32, (count, run), 0)
    matches = jnp.where(shifts == rel, 1.0, 0.0)
    upper = (
        lax.broadcasted_iota(jnp.int32, (run, run), 0)
        <= lax.broadcasted_iota(jnp.int32, (run, run), 1)
    )
    order = jnp.dot(
        matches.astype(jnp.bfloat16),
        jnp.where(upper, 1.0, 0.0).astype(jnp.bfloat16),
        preferred_element_type=jnp.float32,
    )
    rank = jnp.sum(matches * order, axis=0, keepdims=True).astype(jnp.int32) - 1
    slot = rel * cap + rank
    slot_ref[...] = slot
    pos = pos_ref[...]
    which = lax.broadcasted_iota(jnp.int32, (8, run), 0)
    parts = jnp.where(
        which == 0, pos // 32, jnp.where(which == 1, pos % 32, jnp.where(which == 2, 1, 0))
    )
    parts = parts.astype(jnp.float32).astype(jnp.bfloat16)

    def one(shift, carry):
        here = slot == lax.broadcasted_iota(jnp.int32, (cap, run), 0) + shift * cap
        hot = jnp.where(here, 1.0, 0.0).astype(jnp.bfloat16)
        got = lax.dot_general(
            parts, hot, (((1,), (1,)), ((), ())), preferred_element_type=jnp.float32
        )
        place = got[0:1] * 32.0 + got[1:2] + (1.0 - got[2:3]) * run
        place_ref[pl.ds(shift, 1), :] = place.astype(jnp.int32)
        return carry

    lax.fori_loop(0, count, one, 0)


def layer_kernel(
    count, cap, tok_ref, gain_ref, bias_ref, qkv_ref, out_w_ref, idc_ref, idr_ref, slot_ref,
    filled_ref, q_ref, k_ref, v_ref, vis_ref,
):
    run, width = tok_ref.shape
    inner = HEADS * HEAD_DIM
    scale = HEAD_DIM ** (-0.5) * math.log2(math.e)

    def project(block, carry):
        rows = pl.ds(pl.multiple_of(block * ROWS, ROWS), ROWS)
        values = tok_ref[rows, :].astype(jnp.float32)
        center = values - jnp.mean(values, axis=1, keepdims=True)
        spread = jnp.mean(center * center, axis=1, keepdims=True)
        normed = center * lax.rsqrt(spread + 1e-06) * gain_ref[...] + bias_ref[...]
        normed = normed.astype(jnp.bfloat16)
        pad = jnp.zeros((ROWS, LANES - HEAD_DIM), jnp.float32)
        lane = lax.broadcasted_iota(jnp.int32, (ROWS, LANES - HEAD_DIM), 1)
        ones = jnp.where(lane == 0, 1.0, 0.0)
        full = jnp.dot(normed, qkv_ref[...], preferred_element_type=jnp.float32)
        for which, ref in enumerate((q_ref, k_ref, v_ref)):
            for head in range(HEADS):
                start = which * inner + head * HEAD_DIM
                piece = full[:, start : start + HEAD_DIM]
                if which == 0:
                    piece = piece * scale
                piece = jnp.concatenate([piece, ones if which == 2 else pad], axis=1)
                ref[head, rows, :] = piece.astype(jnp.bfloat16)
        return carry

    lax.fori_loop(0, run // ROWS, project, 0)

    def attend(block, carry):
        rows = pl.ds(pl.multiple_of(block * ROWS, ROWS), ROWS)
        mask = jnp.where(idc_ref[rows, :] == idr_ref[...], 0.0, masked_fill)
        pieces = []
        for head in range(HEADS):
            scores = lax.dot_general(
                q_ref[head, rows, :], k_ref[head], (((1,), (1,)), ((), ())),
                preferred_element_type=jnp.float32,
            ) + mask
            top = jnp.max(scores, axis=1, keepdims=True)
            weights = jnp.exp2(scores - top).astype(jnp.bfloat16)
            summed = jnp.dot(weights, v_ref[head], preferred_element_type=jnp.float32)
            pieces.append(summed[:, :HEAD_DIM] / summed[:, HEAD_DIM : HEAD_DIM + 1])
        attended = jnp.concatenate(pieces, axis=1).astype(jnp.bfloat16)
        mixed = jnp.dot(attended, out_w_ref[...], preferred_element_type=jnp.float32)
        vis_ref[rows, :] = (tok_ref[rows, :].astype(jnp.float32) + mixed).astype(jnp.bfloat16)
        return carry

    lax.fori_loop(0, run // ROWS, attend, 0)

    def pack(shift, carry):
        slot = slot_ref[...]
        lanes = lax.broadcasted_iota(jnp.int32, (cap, run), 0) + shift * cap
        here = slot == lanes
        any_here = jnp.max(jnp.where(slot // cap == shift, 1, 0)) > 0
        rows = pl.ds(pl.multiple_of(shift * cap, cap), cap)

        @pl.when(any_here)
        def _():
            hot = jnp.where(here, 1.0, 0.0).astype(jnp.bfloat16)
            filled_ref[rows, :] = jnp.dot(
                hot, vis_ref[...], preferred_element_type=jnp.float32
            ).astype(jnp.bfloat16)

        @pl.when(jnp.logical_not(any_here))
        def _():
            filled_ref[rows, :] = jnp.zeros((cap, width), jnp.bfloat16)

        return carry

    lax.fori_loop(0, count, pack, 0)


def unpack_kernel(count, cap, place_ref, flag_ref, at_ref, *refs):
    blocks, (out_ref, held_ref, held_place, acc_ref, sems) = refs[:count], refs[count:]
    run = out_ref.shape[0]
    for shift in range(count):
        @pl.when(flag_ref[shift] > 0)
        def _(shift=shift):
            at = at_ref[shift]
            pltpu.make_async_copy(blocks[shift], held_ref.at[at], sems.at[at]).start()
            held_place[pl.ds(at, 1), :] = place_ref[shift : shift + 1, :]

    acc_ref[...] = jnp.zeros_like(acc_ref)

    def one(at, carry):
        pltpu.make_async_copy(blocks[0], held_ref.at[at], sems.at[at]).wait()
        hot = held_place[pl.ds(at, 1), :] == lax.broadcasted_iota(jnp.int32, (run, cap), 0)
        acc_ref[...] += jnp.dot(
            jnp.where(hot, 1.0, 0.0).astype(jnp.bfloat16), held_ref[at],
            preferred_element_type=jnp.float32,
        )
        return carry

    lax.fori_loop(0, run // cap, one, 0)
    out_ref[...] = acc_ref[...].astype(out_ref.dtype)


def local(tokens, norm_gain, norm_bias, qkv_weight, out_weight, segment_ids, dest_map):
    run, width = tokens.shape
    count = lax.axis_size("seq")
    me = lax.axis_index("seq")
    cap = run * 2 // count
    rel = (dest_map // run - me + count) % count
    slot, places = pl.pallas_call(
        functools.partial(route_kernel, count, cap),
        out_shape=(
            jax.ShapeDtypeStruct((1, run), jnp.int32),
            jax.ShapeDtypeStruct((count, cap), jnp.int32),
        ),
        in_specs=[VMEM] * 2,
        out_specs=(VMEM, VMEM),
    )(rel[None], (dest_map % run)[None])
    gathered = lax.all_gather(places, "seq")
    shifts = jnp.arange(count)
    my_places = gathered[(me - shifts + count) % count, shifts]
    needed = jnp.any(gathered[:, :, 0] < run, axis=0)
    flags = (my_places[:, 0] < run).astype(jnp.int32)
    at = jnp.sum(jnp.where(shifts[None] < shifts[:, None], flags[None], 0), axis=1)

    filled = pl.pallas_call(
        functools.partial(layer_kernel, count, cap),
        out_shape=jax.ShapeDtypeStruct((count * cap, width), jnp.bfloat16),
        in_specs=[VMEM] * 8,
        out_specs=VMEM,
        scratch_shapes=[pltpu.VMEM((HEADS, run, LANES), jnp.bfloat16)] * 3
        + [pltpu.VMEM((run, width), jnp.bfloat16)],
        compiler_params=pltpu.CompilerParams(vmem_limit_bytes=56 * 2**20),
        cost_estimate=pl.CostEstimate(
            flops=16 * 10**9, bytes_accessed=12 * 10**6, transcendentals=8 * 10**6
        ),
    )(
        tokens, norm_gain[None], norm_bias[None], qkv_weight, out_weight,
        segment_ids[:, None], segment_ids[None], slot,
    )
    blocks = [filled[:cap]]
    for shift in range(1, count):
        pairs = [(source, (source + shift) % count) for source in range(count)]
        start = shift * cap
        blocks.append(
            lax.cond(
                needed[shift],
                lambda rows, start=start, pairs=pairs: lax.ppermute(
                    rows[start : start + cap], "seq", pairs
                ),
                lambda rows: jnp.zeros((cap, width), jnp.bfloat16),
                filled,
            )
        )
    return pl.pallas_call(
        functools.partial(unpack_kernel, count, cap),
        out_shape=jax.ShapeDtypeStruct((run, width), jnp.bfloat16),
        in_specs=[VMEM]
        + [pl.BlockSpec(memory_space=pltpu.SMEM)] * 2
        + [pl.BlockSpec(memory_space=pl.ANY)] * count,
        out_specs=VMEM,
        scratch_shapes=[
            pltpu.VMEM((run // cap, cap, width), jnp.bfloat16),
            pltpu.VMEM((run // cap, cap), jnp.int32),
            pltpu.VMEM((run, width), jnp.float32),
            pltpu.SemaphoreType.DMA((run // cap,)),
        ],
        compiler_params=pltpu.CompilerParams(vmem_limit_bytes=40 * 2**20),
    )(my_places, flags, at, *blocks)


def solution(mesh):
    placed = (P(("dp", "seq"), None), P(), P(), P(), P(), P(("dp", "seq")), P(("dp", "seq")))
    return jax.shard_map(
        local, mesh=mesh, in_specs=placed, out_specs=P(("dp", "seq"), None), check_vma=False
    )
```

```python
import functools
import math

import jax
import jax.numpy as jnp
from jax import lax
from jax.experimental import pallas as pl
from jax.experimental.pallas import tpu as pltpu
from jax.sharding import PartitionSpec as P

HEADS = 8
HEAD_DIM = 72
LANES = 128
ROWS = 256
VMEM = pl.BlockSpec(memory_space=pltpu.VMEM)
masked_fill = -1e30


def route_kernel(
    count, cap, dest_ref, slot_ref, mine_ref, needed_ref, place_ref, all_ref, send_sems, recv_sems
):
    run = dest_ref.shape[1]
    me = lax.axis_index("seq")

    barrier = pltpu.get_barrier_semaphore()

    def greet(step, carry):
        pl.semaphore_signal(
            barrier, inc=1, device_id={"seq": lax.rem(me + step, count)},
            device_id_type=pl.DeviceIdType.MESH,
        )
        return carry

    lax.fori_loop(1, count, greet, 0)
    rel = lax.rem(dest_ref[...] // run - me + count, count)
    shifts = lax.broadcasted_iota(jnp.int32, (count, run), 0)
    matches = jnp.where(shifts == rel, 1.0, 0.0)
    upper = (
        lax.broadcasted_iota(jnp.int32, (run, run), 0)
        <= lax.broadcasted_iota(jnp.int32, (run, run), 1)
    )
    order = jnp.dot(
        matches.astype(jnp.bfloat16),
        jnp.where(upper, 1.0, 0.0).astype(jnp.bfloat16),
        preferred_element_type=jnp.float32,
    )
    rank = jnp.sum(matches * order, axis=0, keepdims=True).astype(jnp.int32) - 1
    slot = rel * cap + rank
    slot_ref[...] = slot
    pos = dest_ref[...] % run
    which = lax.broadcasted_iota(jnp.int32, (8, run), 0)
    parts = jnp.where(
        which == 0, pos // 32, jnp.where(which == 1, pos % 32, jnp.where(which == 2, 1, 0))
    )
    parts = parts.astype(jnp.float32).astype(jnp.bfloat16)

    def one(shift, carry):
        here = slot == lax.broadcasted_iota(jnp.int32, (cap, run), 0) + shift * cap
        hot = jnp.where(here, 1.0, 0.0).astype(jnp.bfloat16)
        got = lax.dot_general(
            parts, hot, (((1,), (1,)), ((), ())), preferred_element_type=jnp.float32
        )
        place = got[0:1] * 32.0 + got[1:2] + (1.0 - got[2:3]) * run
        place_ref[pl.ds(shift, 1), :] = place.astype(jnp.int32)
        return carry

    lax.fori_loop(0, count, one, 0)
    pl.semaphore_wait(barrier, count - 1)

    def copy(step):
        return pltpu.make_async_remote_copy(
            src_ref=place_ref,
            dst_ref=all_ref.at[step],
            send_sem=send_sems.at[step],
            recv_sem=recv_sems.at[step],
            device_id={"seq": lax.rem(me + step, count)},
            device_id_type=pl.DeviceIdType.MESH,
        )

    def send(step, carry):
        copy(step).start()
        return carry

    def wait(step, carry):
        copy(step).wait()
        return carry

    lax.fori_loop(1, count, send, 0)
    lax.fori_loop(1, count, wait, 0)
    least = place_ref[...]
    mine_ref[0:1, :] = place_ref[0:1, :]

    def take(step, least):
        mine_ref[pl.ds(step, 1), :] = all_ref[step, pl.ds(step, 1), :]
        return jnp.minimum(least, all_ref[step])

    least = lax.fori_loop(1, count, take, least)
    used = jnp.max(jnp.where(least < run, 1, 0), axis=1, keepdims=True)
    needed_ref[...] = jnp.broadcast_to(used, needed_ref.shape)


def layer_kernel(
    count, cap, tok_ref, gain_ref, bias_ref, qkv_ref, out_w_ref, ids_ref, slot_ref, *refs
):
    outs, (filled_ref, q_ref, k_ref, v_ref, vis_ref, sems) = refs[:count], refs[count:]
    run, width = tok_ref.shape
    inner = HEADS * HEAD_DIM
    scale = HEAD_DIM ** (-0.5) * math.log2(math.e)

    def project(block, carry):
        rows = pl.ds(pl.multiple_of(block * ROWS, ROWS), ROWS)
        values = tok_ref[rows, :].astype(jnp.float32)
        center = values - jnp.mean(values, axis=1, keepdims=True)
        spread = jnp.mean(center * center, axis=1, keepdims=True)
        normed = center * lax.rsqrt(spread + 1e-06) * gain_ref[...][None] + bias_ref[...][None]
        normed = normed.astype(jnp.bfloat16)
        pad = jnp.zeros((ROWS, LANES - HEAD_DIM), jnp.float32)
        lane = lax.broadcasted_iota(jnp.int32, (ROWS, LANES - HEAD_DIM), 1)
        ones = jnp.where(lane == 0, 1.0, 0.0)
        full = lax.dot_general(
            normed, qkv_ref[...], (((1,), (1,)), ((), ())), preferred_element_type=jnp.float32
        )
        for which, ref in enumerate((q_ref, k_ref, v_ref)):
            for head in range(HEADS):
                start = which * inner + head * HEAD_DIM
                piece = full[:, start : start + HEAD_DIM]
                if which == 0:
                    piece = piece * scale
                piece = jnp.concatenate([piece, ones if which == 2 else pad], axis=1)
                ref[head, rows, :] = piece.astype(jnp.bfloat16)
        return carry

    lax.fori_loop(0, run // ROWS, project, 0)

    def attend(block, carry):
        rows = pl.ds(pl.multiple_of(block * ROWS, ROWS), ROWS)
        own = jnp.broadcast_to(ids_ref[:, rows], (8, ROWS)).T[:, :1]
        mask = jnp.where(own == ids_ref[...], 0.0, masked_fill)
        pieces = []
        for head in range(HEADS):
            scores = lax.dot_general(
                q_ref[head, rows, :], k_ref[head], (((1,), (1,)), ((), ())),
                preferred_element_type=jnp.float32,
            ) + mask
            top = jnp.max(scores, axis=1, keepdims=True)
            weights = jnp.exp2(scores - top).astype(jnp.bfloat16)
            summed = jnp.dot(weights, v_ref[head], preferred_element_type=jnp.float32)
            pieces.append(summed[:, :HEAD_DIM] / summed[:, HEAD_DIM : HEAD_DIM + 1])
        attended = jnp.concatenate(pieces, axis=1).astype(jnp.bfloat16)
        mixed = jnp.dot(attended, out_w_ref[...], preferred_element_type=jnp.float32)
        vis_ref[rows, :] = (tok_ref[rows, :].astype(jnp.float32) + mixed).astype(jnp.bfloat16)
        return carry

    lax.fori_loop(0, run // ROWS, attend, 0)

    def pack(shift, carry):
        slot = slot_ref[...]
        lanes = lax.broadcasted_iota(jnp.int32, (cap, run), 0) + shift * cap
        here = slot == lanes
        any_here = jnp.max(jnp.where(here, 1, 0)) > 0

        @pl.when(any_here)
        def _():
            hot = jnp.where(here, 1.0, 0.0).astype(jnp.bfloat16)
            filled_ref[shift] = jnp.dot(
                hot, vis_ref[...], preferred_element_type=jnp.float32
            ).astype(jnp.bfloat16)

        @pl.when(jnp.logical_not(any_here))
        def _():
            filled_ref[shift] = jnp.zeros((cap, width), jnp.bfloat16)

        return carry

    lax.fori_loop(0, count, pack, 0)
    copies = [
        pltpu.make_async_copy(filled_ref.at[shift], outs[shift], sems.at[shift])
        for shift in range(count)
    ]
    for copy in copies:
        copy.start()
    for copy in copies:
        copy.wait()


def unpack_kernel(count, cap, place_ref, *refs):
    blocks, (out_ref, held_ref, held_place, acc_ref, sems) = refs[:count], refs[count:]
    run = out_ref.shape[0]
    at = jnp.int32(0)
    for shift in range(count):
        used = (jnp.min(place_ref[shift : shift + 1, :]) < run).astype(jnp.int32)

        @pl.when(used > 0)
        def _(shift=shift, at=at):
            pltpu.make_async_copy(blocks[shift], held_ref.at[at], sems.at[at]).start()
            held_place[pl.ds(at, 1), :] = place_ref[shift : shift + 1, :]

        at = at + used

    acc_ref[...] = jnp.zeros_like(acc_ref)

    def one(at, carry):
        pltpu.make_async_copy(blocks[0], held_ref.at[at], sems.at[at]).wait()
        hot = held_place[pl.ds(at, 1), :] == lax.broadcasted_iota(jnp.int32, (run, cap), 0)
        acc_ref[...] += jnp.dot(
            jnp.where(hot, 1.0, 0.0).astype(jnp.bfloat16), held_ref[at],
            preferred_element_type=jnp.float32,
        )
        return carry

    lax.fori_loop(0, run // cap, one, 0)
    out_ref[...] = acc_ref[...].astype(out_ref.dtype)


def local(tokens, norm_gain, norm_bias, qkv_weight, out_weight, segment_ids, dest_map):
    run, width = tokens.shape
    count = lax.axis_size("seq")
    cap = run * 2 // count
    slot, my_places, needed = pl.pallas_call(
        functools.partial(route_kernel, count, cap),
        out_shape=(
            jax.ShapeDtypeStruct((1, run), jnp.int32),
            jax.ShapeDtypeStruct((count, cap), jnp.int32),
            jax.ShapeDtypeStruct((count, LANES), jnp.int32),
        ),
        in_specs=[VMEM],
        out_specs=(VMEM,) * 3,
        scratch_shapes=[
            pltpu.VMEM((count, cap), jnp.int32),
            pltpu.VMEM((count, count, cap), jnp.int32),
            pltpu.SemaphoreType.DMA((count,)),
            pltpu.SemaphoreType.DMA((count,)),
        ],
        compiler_params=pltpu.CompilerParams(
            collective_id=0, has_side_effects=True, vmem_limit_bytes=24 * 2**20
        ),
    )(dest_map[None])

    blocks = pl.pallas_call(
        functools.partial(layer_kernel, count, cap),
        out_shape=(jax.ShapeDtypeStruct((cap, width), jnp.bfloat16),) * count,
        in_specs=[VMEM] * 7,
        out_specs=(pl.BlockSpec(memory_space=pl.ANY),) * count,
        scratch_shapes=[pltpu.VMEM((count, cap, width), jnp.bfloat16)]
        + [pltpu.VMEM((HEADS, run, LANES), jnp.bfloat16)] * 3
        + [pltpu.VMEM((run, width), jnp.bfloat16), pltpu.SemaphoreType.DMA((count,))],
        compiler_params=pltpu.CompilerParams(vmem_limit_bytes=56 * 2**20),
        cost_estimate=pl.CostEstimate(
            flops=16 * 10**9, bytes_accessed=12 * 10**6, transcendentals=8 * 10**6
        ),
    )(
        tokens, norm_gain, norm_bias, qkv_weight.T, out_weight, segment_ids[None], slot,
    )
    blocks = list(blocks)
    for shift in range(1, count):
        pairs = [(source, (source + shift) % count) for source in range(count)]
        blocks[shift] = lax.cond(
            needed[shift, 0] > 0,
            lambda rows, pairs=pairs: lax.ppermute(rows, "seq", pairs),
            lambda rows: rows,
            blocks[shift],
        )
    return pl.pallas_call(
        functools.partial(unpack_kernel, count, cap),
        out_shape=jax.ShapeDtypeStruct((run, width), jnp.bfloat16),
        in_specs=[VMEM]
        + [pl.BlockSpec(memory_space=pl.ANY)] * count,
        out_specs=VMEM,
        scratch_shapes=[
            pltpu.VMEM((run // cap, cap, width), jnp.bfloat16),
            pltpu.VMEM((run // cap, cap), jnp.int32),
            pltpu.VMEM((run, width), jnp.float32),
            pltpu.SemaphoreType.DMA((run // cap,)),
        ],
        compiler_params=pltpu.CompilerParams(vmem_limit_bytes=40 * 2**20),
    )(my_places, *blocks)


def solution(mesh):
    placed = (P(("dp", "seq"), None), P(), P(), P(), P(), P(("dp", "seq")), P(("dp", "seq")))
    return jax.shard_map(
        local, mesh=mesh, in_specs=placed, out_specs=P(("dp", "seq"), None), check_vma=False
    )
```

```python
import functools
import math

import jax
import jax.numpy as jnp
from jax import lax
from jax.experimental import pallas as pl
from jax.experimental.pallas import tpu as pltpu
from jax.sharding import PartitionSpec as P

HEADS = 8
HEAD_DIM = 72
LANES = 128
ROWS = 256
VMEM = pl.BlockSpec(memory_space=pltpu.VMEM)
masked_fill = -1e30


def route_kernel(
    count, cap, dest_ref, slot_ref, mine_ref, needed_ref, place_ref, all_ref, send_sems, recv_sems
):
    run = dest_ref.shape[1]
    me = lax.axis_index("seq")

    barrier = pltpu.get_barrier_semaphore()

    def greet(step, carry):
        pl.semaphore_signal(
            barrier, inc=1, device_id={"seq": lax.rem(me + step, count)},
            device_id_type=pl.DeviceIdType.MESH,
        )
        return carry

    lax.fori_loop(1, count, greet, 0)
    rel = lax.rem(dest_ref[...] // run - me + count, count)
    shifts = lax.broadcasted_iota(jnp.int32, (count, run), 0)
    matches = jnp.where(shifts == rel, 1.0, 0.0)
    upper = (
        lax.broadcasted_iota(jnp.int32, (run, run), 0)
        <= lax.broadcasted_iota(jnp.int32, (run, run), 1)
    )
    order = jnp.dot(
        matches.astype(jnp.bfloat16),
        jnp.where(upper, 1.0, 0.0).astype(jnp.bfloat16),
        preferred_element_type=jnp.float32,
    )
    rank = jnp.sum(matches * order, axis=0, keepdims=True).astype(jnp.int32) - 1
    slot = rel * cap + rank
    slot_ref[...] = slot
    pos = dest_ref[...] % run
    which = lax.broadcasted_iota(jnp.int32, (8, run), 0)
    parts = jnp.where(
        which == 0, pos // 32, jnp.where(which == 1, pos % 32, jnp.where(which == 2, 1, 0))
    )
    parts = parts.astype(jnp.float32).astype(jnp.bfloat16)

    def one(shift, carry):
        here = slot == lax.broadcasted_iota(jnp.int32, (cap, run), 0) + shift * cap
        hot = jnp.where(here, 1.0, 0.0).astype(jnp.bfloat16)
        got = lax.dot_general(
            parts, hot, (((1,), (1,)), ((), ())), preferred_element_type=jnp.float32
        )
        place = got[0:1] * 32.0 + got[1:2] + (1.0 - got[2:3]) * run
        place_ref[pl.ds(shift, 1), :] = place.astype(jnp.int32)
        return carry

    lax.fori_loop(0, count, one, 0)
    pl.semaphore_wait(barrier, count - 1)

    def copy(step):
        return pltpu.make_async_remote_copy(
            src_ref=place_ref,
            dst_ref=all_ref.at[step],
            send_sem=send_sems.at[step],
            recv_sem=recv_sems.at[step],
            device_id={"seq": lax.rem(me + step, count)},
            device_id_type=pl.DeviceIdType.MESH,
        )

    def send(step, carry):
        copy(step).start()
        return carry

    def wait(step, carry):
        copy(step).wait()
        return carry

    lax.fori_loop(1, count, send, 0)
    lax.fori_loop(1, count, wait, 0)
    least = place_ref[...]
    mine_ref[0:1, :] = place_ref[0:1, :]

    def take(step, least):
        mine_ref[pl.ds(step, 1), :] = all_ref[step, pl.ds(step, 1), :]
        return jnp.minimum(least, all_ref[step])

    least = lax.fori_loop(1, count, take, least)
    used = jnp.max(jnp.where(least < run, 1, 0), axis=1, keepdims=True)
    needed_ref[...] = jnp.broadcast_to(used, needed_ref.shape)


def layer_kernel(
    count, cap, tok_ref, gain_ref, bias_ref, qkv_ref, out_w_ref, ids_ref, slot_ref, *refs
):
    outs, (filled_ref, q_ref, k_ref, v_ref, vis_ref, sems) = refs[:count], refs[count:]
    run, width = tok_ref.shape
    inner = HEADS * HEAD_DIM
    scale = HEAD_DIM ** (-0.5) * math.log2(math.e)

    def project(block, carry):
        rows = pl.ds(pl.multiple_of(block * ROWS, ROWS), ROWS)
        values = tok_ref[rows, :].astype(jnp.float32)
        center = values - jnp.mean(values, axis=1, keepdims=True)
        spread = jnp.mean(center * center, axis=1, keepdims=True)
        normed = center * lax.rsqrt(spread + 1e-06) * gain_ref[...][None] + bias_ref[...][None]
        normed = normed.astype(jnp.bfloat16)
        pad = jnp.zeros((ROWS, LANES - HEAD_DIM), jnp.float32)
        lane = lax.broadcasted_iota(jnp.int32, (ROWS, LANES - HEAD_DIM), 1)
        ones = jnp.where(lane == 0, 1.0, 0.0)
        full = lax.dot_general(
            normed, qkv_ref[...], (((1,), (1,)), ((), ())), preferred_element_type=jnp.float32
        )
        for which, ref in enumerate((q_ref, k_ref, v_ref)):
            for head in range(HEADS):
                start = which * inner + head * HEAD_DIM
                piece = full[:, start : start + HEAD_DIM]
                if which == 0:
                    piece = piece * scale
                piece = jnp.concatenate([piece, ones if which == 2 else pad], axis=1)
                ref[head, rows, :] = piece.astype(jnp.bfloat16)
        return carry

    lax.fori_loop(0, run // ROWS, project, 0)

    def attend(block, carry):
        rows = pl.ds(pl.multiple_of(block * ROWS, ROWS), ROWS)
        own = jnp.broadcast_to(ids_ref[:, rows], (8, ROWS)).T[:, :1]
        mask = jnp.where(own == ids_ref[...], 0.0, masked_fill)
        pieces = []
        for head in range(HEADS):
            scores = lax.dot_general(
                q_ref[head, rows, :], k_ref[head], (((1,), (1,)), ((), ())),
                preferred_element_type=jnp.float32,
            ) + mask
            top = jnp.max(scores, axis=1, keepdims=True)
            weights = jnp.exp2((scores - top).astype(jnp.bfloat16))
            summed = jnp.dot(weights, v_ref[head], preferred_element_type=jnp.float32)
            pieces.append(summed[:, :HEAD_DIM] / summed[:, HEAD_DIM : HEAD_DIM + 1])
        attended = jnp.concatenate(pieces, axis=1).astype(jnp.bfloat16)
        mixed = jnp.dot(attended, out_w_ref[...], preferred_element_type=jnp.float32)
        vis_ref[rows, :] = (tok_ref[rows, :].astype(jnp.float32) + mixed).astype(jnp.bfloat16)
        return carry

    lax.fori_loop(0, run // ROWS, attend, 0)

    def pack(shift, carry):
        slot = slot_ref[...]
        lanes = lax.broadcasted_iota(jnp.int32, (cap, run), 0) + shift * cap
        here = slot == lanes
        any_here = jnp.max(jnp.where(here, 1, 0)) > 0

        @pl.when(any_here)
        def _():
            hot = jnp.where(here, 1.0, 0.0).astype(jnp.bfloat16)
            filled_ref[shift] = jnp.dot(
                hot, vis_ref[...], preferred_element_type=jnp.float32
            ).astype(jnp.bfloat16)

        @pl.when(jnp.logical_not(any_here))
        def _():
            filled_ref[shift] = jnp.zeros((cap, width), jnp.bfloat16)

        return carry

    lax.fori_loop(0, count, pack, 0)
    copies = [
        pltpu.make_async_copy(filled_ref.at[shift], outs[shift], sems.at[shift])
        for shift in range(count)
    ]
    for copy in copies:
        copy.start()
    for copy in copies:
        copy.wait()


def unpack_kernel(count, cap, place_ref, *refs):
    blocks, (out_ref, held_ref, held_place, acc_ref, sems) = refs[:count], refs[count:]
    run = out_ref.shape[0]
    at = jnp.int32(0)
    for shift in range(count):
        used = (jnp.min(place_ref[shift : shift + 1, :]) < run).astype(jnp.int32)

        @pl.when(used > 0)
        def _(shift=shift, at=at):
            pltpu.make_async_copy(blocks[shift], held_ref.at[at], sems.at[at]).start()
            held_place[pl.ds(at, 1), :] = place_ref[shift : shift + 1, :]

        at = at + used

    acc_ref[...] = jnp.zeros_like(acc_ref)

    def one(at, carry):
        pltpu.make_async_copy(blocks[0], held_ref.at[at], sems.at[at]).wait()
        hot = held_place[pl.ds(at, 1), :] == lax.broadcasted_iota(jnp.int32, (run, cap), 0)
        acc_ref[...] += jnp.dot(
            jnp.where(hot, 1.0, 0.0).astype(jnp.bfloat16), held_ref[at],
            preferred_element_type=jnp.float32,
        )
        return carry

    lax.fori_loop(0, run // cap, one, 0)
    out_ref[...] = acc_ref[...].astype(out_ref.dtype)


def local(tokens, norm_gain, norm_bias, qkv_weight, out_weight, segment_ids, dest_map):
    run, width = tokens.shape
    count = lax.axis_size("seq")
    cap = run * 2 // count
    slot, my_places, needed = pl.pallas_call(
        functools.partial(route_kernel, count, cap),
        out_shape=(
            jax.ShapeDtypeStruct((1, run), jnp.int32),
            jax.ShapeDtypeStruct((count, cap), jnp.int32),
            jax.ShapeDtypeStruct((count, LANES), jnp.int32),
        ),
        in_specs=[VMEM],
        out_specs=(VMEM,) * 3,
        scratch_shapes=[
            pltpu.VMEM((count, cap), jnp.int32),
            pltpu.VMEM((count, count, cap), jnp.int32),
            pltpu.SemaphoreType.DMA((count,)),
            pltpu.SemaphoreType.DMA((count,)),
        ],
        compiler_params=pltpu.CompilerParams(
            collective_id=0, has_side_effects=True, vmem_limit_bytes=24 * 2**20
        ),
    )(dest_map[None])

    blocks = pl.pallas_call(
        functools.partial(layer_kernel, count, cap),
        out_shape=(jax.ShapeDtypeStruct((cap, width), jnp.bfloat16),) * count,
        in_specs=[VMEM] * 7,
        out_specs=(pl.BlockSpec(memory_space=pl.ANY),) * count,
        scratch_shapes=[pltpu.VMEM((count, cap, width), jnp.bfloat16)]
        + [pltpu.VMEM((HEADS, run, LANES), jnp.bfloat16)] * 3
        + [pltpu.VMEM((run, width), jnp.bfloat16), pltpu.SemaphoreType.DMA((count,))],
        compiler_params=pltpu.CompilerParams(vmem_limit_bytes=56 * 2**20),
        cost_estimate=pl.CostEstimate(
            flops=16 * 10**9, bytes_accessed=12 * 10**6, transcendentals=8 * 10**6
        ),
    )(
        tokens, norm_gain, norm_bias, qkv_weight.T, out_weight, segment_ids[None], slot,
    )
    blocks = list(blocks)
    for shift in range(1, count):
        pairs = [(source, (source + shift) % count) for source in range(count)]
        blocks[shift] = lax.cond(
            needed[shift, 0] > 0,
            lambda rows, pairs=pairs: lax.ppermute(rows, "seq", pairs),
            lambda rows: rows,
            blocks[shift],
        )
    return pl.pallas_call(
        functools.partial(unpack_kernel, count, cap),
        out_shape=jax.ShapeDtypeStruct((run, width), jnp.bfloat16),
        in_specs=[VMEM]
        + [pl.BlockSpec(memory_space=pl.ANY)] * count,
        out_specs=VMEM,
        scratch_shapes=[
            pltpu.VMEM((run // cap, cap, width), jnp.bfloat16),
            pltpu.VMEM((run // cap, cap), jnp.int32),
            pltpu.VMEM((run, width), jnp.float32),
            pltpu.SemaphoreType.DMA((run // cap,)),
        ],
        compiler_params=pltpu.CompilerParams(vmem_limit_bytes=40 * 2**20),
    )(my_places, *blocks)


def solution(mesh):
    placed = (P(("dp", "seq"), None), P(), P(), P(), P(), P(("dp", "seq")), P(("dp", "seq")))
    return jax.shard_map(
        local, mesh=mesh, in_specs=placed, out_specs=P(("dp", "seq"), None), check_vma=False
    )
```

```python
import functools
import math

import jax
import jax.numpy as jnp
from jax import lax
from jax.experimental import pallas as pl
from jax.experimental.pallas import tpu as pltpu
from jax.sharding import PartitionSpec as P

HEADS = 8
HEAD_DIM = 72
LANES = 128
ROWS = 256
SPAN = 512
VMEM = pl.BlockSpec(memory_space=pltpu.VMEM)
masked_fill = -1e30


def route_kernel(
    count, cap, dest_ref, slot_ref, mine_ref, needed_ref, place_ref, all_ref, send_sems, recv_sems
):
    run = dest_ref.shape[1]
    me = lax.axis_index("seq")

    barrier = pltpu.get_barrier_semaphore()

    def greet(step, carry):
        pl.semaphore_signal(
            barrier, inc=1, device_id={"seq": lax.rem(me + step, count)},
            device_id_type=pl.DeviceIdType.MESH,
        )
        return carry

    lax.fori_loop(1, count, greet, 0)
    rel = lax.rem(dest_ref[...] // run - me + count, count)
    shifts = lax.broadcasted_iota(jnp.int32, (count, run), 0)
    matches = jnp.where(shifts == rel, 1.0, 0.0)
    upper = (
        lax.broadcasted_iota(jnp.int32, (run, run), 0)
        <= lax.broadcasted_iota(jnp.int32, (run, run), 1)
    )
    order = jnp.dot(
        matches.astype(jnp.bfloat16),
        jnp.where(upper, 1.0, 0.0).astype(jnp.bfloat16),
        preferred_element_type=jnp.float32,
    )
    rank = jnp.sum(matches * order, axis=0, keepdims=True).astype(jnp.int32) - 1
    slot = rel * cap + rank
    slot_ref[...] = slot
    pos = dest_ref[...] % run
    which = lax.broadcasted_iota(jnp.int32, (8, run), 0)
    parts = jnp.where(
        which == 0, pos // 32, jnp.where(which == 1, pos % 32, jnp.where(which == 2, 1, 0))
    )
    parts = parts.astype(jnp.float32).astype(jnp.bfloat16)

    def one(shift, carry):
        here = slot == lax.broadcasted_iota(jnp.int32, (cap, run), 0) + shift * cap
        hot = jnp.where(here, 1.0, 0.0).astype(jnp.bfloat16)
        got = lax.dot_general(
            parts, hot, (((1,), (1,)), ((), ())), preferred_element_type=jnp.float32
        )
        place = got[0:1] * 32.0 + got[1:2] + (1.0 - got[2:3]) * run
        place_ref[pl.ds(shift, 1), :] = place.astype(jnp.int32)
        return carry

    lax.fori_loop(0, count, one, 0)
    pl.semaphore_wait(barrier, count - 1)

    def copy(step):
        return pltpu.make_async_remote_copy(
            src_ref=place_ref,
            dst_ref=all_ref.at[step],
            send_sem=send_sems.at[step],
            recv_sem=recv_sems.at[step],
            device_id={"seq": lax.rem(me + step, count)},
            device_id_type=pl.DeviceIdType.MESH,
        )

    def send(step, carry):
        copy(step).start()
        return carry

    def wait(step, carry):
        copy(step).wait()
        return carry

    lax.fori_loop(1, count, send, 0)
    lax.fori_loop(1, count, wait, 0)
    least = place_ref[...]
    mine_ref[0:1, :] = place_ref[0:1, :]

    def take(step, least):
        mine_ref[pl.ds(step, 1), :] = all_ref[step, pl.ds(step, 1), :]
        return jnp.minimum(least, all_ref[step])

    least = lax.fori_loop(1, count, take, least)
    used = jnp.max(jnp.where(least < run, 1, 0), axis=1, keepdims=True)
    needed_ref[...] = jnp.broadcast_to(used, needed_ref.shape)


def layer_kernel(
    count, cap, tok_ref, gain_ref, bias_ref, qkv_ref, out_w_ref, ids_ref, slot_ref, *refs
):
    outs, (filled_ref, q_ref, k_ref, v_ref, vis_ref, sems) = refs[:count], refs[count:]
    run, width = tok_ref.shape
    inner = HEADS * HEAD_DIM
    scale = HEAD_DIM ** (-0.5) * math.log2(math.e)

    def project(block, carry):
        rows = pl.ds(pl.multiple_of(block * ROWS, ROWS), ROWS)
        values = tok_ref[rows, :].astype(jnp.float32)
        center = values - jnp.mean(values, axis=1, keepdims=True)
        spread = jnp.mean(center * center, axis=1, keepdims=True)
        normed = center * lax.rsqrt(spread + 1e-06) * gain_ref[...][None] + bias_ref[...][None]
        normed = normed.astype(jnp.bfloat16)
        pad = jnp.zeros((ROWS, LANES - HEAD_DIM), jnp.float32)
        lane = lax.broadcasted_iota(jnp.int32, (ROWS, LANES - HEAD_DIM), 1)
        ones = jnp.where(lane == 0, 1.0, 0.0)
        full = lax.dot_general(
            normed, qkv_ref[...], (((1,), (1,)), ((), ())), preferred_element_type=jnp.float32
        )
        for which, ref in enumerate((q_ref, k_ref, v_ref)):
            for head in range(HEADS):
                start = which * inner + head * HEAD_DIM
                piece = full[:, start : start + HEAD_DIM]
                if which == 0:
                    piece = piece * scale
                piece = jnp.concatenate([piece, ones if which == 2 else pad], axis=1)
                ref[head, rows, :] = piece.astype(jnp.bfloat16)
        return carry

    lax.fori_loop(0, run // ROWS, project, 0)

    def attend(block, carry):
        rows = pl.ds(pl.multiple_of(block * SPAN, SPAN), SPAN)
        own = jnp.broadcast_to(ids_ref[:, rows], (8, SPAN)).T[:, :1]
        mask = jnp.where(own == ids_ref[...], 0.0, masked_fill)
        pieces = []
        for head in range(HEADS):
            scores = lax.dot_general(
                q_ref[head, rows, :], k_ref[head], (((1,), (1,)), ((), ())),
                preferred_element_type=jnp.float32,
            ) + mask
            top = jnp.max(scores, axis=1, keepdims=True)
            weights = jnp.exp2((scores - top).astype(jnp.bfloat16))
            summed = jnp.dot(weights, v_ref[head], preferred_element_type=jnp.float32)
            pieces.append(summed[:, :HEAD_DIM] / summed[:, HEAD_DIM : HEAD_DIM + 1])
        attended = jnp.concatenate(pieces, axis=1).astype(jnp.bfloat16)
        mixed = jnp.dot(attended, out_w_ref[...], preferred_element_type=jnp.float32)
        vis_ref[rows, :] = (tok_ref[rows, :].astype(jnp.float32) + mixed).astype(jnp.bfloat16)
        return carry

    lax.fori_loop(0, run // SPAN, attend, 0)

    def pack(shift, carry):
        slot = slot_ref[...]
        lanes = lax.broadcasted_iota(jnp.int32, (cap, run), 0) + shift * cap
        here = slot == lanes
        any_here = jnp.max(jnp.where(here, 1, 0)) > 0

        @pl.when(any_here)
        def _():
            hot = jnp.where(here, 1.0, 0.0).astype(jnp.bfloat16)
            filled_ref[shift] = jnp.dot(
                hot, vis_ref[...], preferred_element_type=jnp.float32
            ).astype(jnp.bfloat16)

        @pl.when(jnp.logical_not(any_here))
        def _():
            filled_ref[shift] = jnp.zeros((cap, width), jnp.bfloat16)

        return carry

    lax.fori_loop(0, count, pack, 0)
    copies = [
        pltpu.make_async_copy(filled_ref.at[shift], outs[shift], sems.at[shift])
        for shift in range(count)
    ]
    for copy in copies:
        copy.start()
    for copy in copies:
        copy.wait()


def unpack_kernel(count, cap, place_ref, *refs):
    blocks, (out_ref, held_ref, held_place, acc_ref, sems) = refs[:count], refs[count:]
    run = out_ref.shape[0]
    at = jnp.int32(0)
    for shift in range(count):
        used = (jnp.min(place_ref[shift : shift + 1, :]) < run).astype(jnp.int32)

        @pl.when(used > 0)
        def _(shift=shift, at=at):
            pltpu.make_async_copy(blocks[shift], held_ref.at[at], sems.at[at]).start()
            held_place[pl.ds(at, 1), :] = place_ref[shift : shift + 1, :]

        at = at + used

    acc_ref[...] = jnp.zeros_like(acc_ref)

    def one(at, carry):
        pltpu.make_async_copy(blocks[0], held_ref.at[at], sems.at[at]).wait()
        hot = held_place[pl.ds(at, 1), :] == lax.broadcasted_iota(jnp.int32, (run, cap), 0)
        acc_ref[...] += jnp.dot(
            jnp.where(hot, 1.0, 0.0).astype(jnp.bfloat16), held_ref[at],
            preferred_element_type=jnp.float32,
        )
        return carry

    lax.fori_loop(0, run // cap, one, 0)
    out_ref[...] = acc_ref[...].astype(out_ref.dtype)


def local(tokens, norm_gain, norm_bias, qkv_weight, out_weight, segment_ids, dest_map):
    run, width = tokens.shape
    count = lax.axis_size("seq")
    cap = run * 2 // count
    slot, my_places, needed = pl.pallas_call(
        functools.partial(route_kernel, count, cap),
        out_shape=(
            jax.ShapeDtypeStruct((1, run), jnp.int32),
            jax.ShapeDtypeStruct((count, cap), jnp.int32),
            jax.ShapeDtypeStruct((count, LANES), jnp.int32),
        ),
        in_specs=[VMEM],
        out_specs=(VMEM,) * 3,
        scratch_shapes=[
            pltpu.VMEM((count, cap), jnp.int32),
            pltpu.VMEM((count, count, cap), jnp.int32),
            pltpu.SemaphoreType.DMA((count,)),
            pltpu.SemaphoreType.DMA((count,)),
        ],
        compiler_params=pltpu.CompilerParams(
            collective_id=0, has_side_effects=True, vmem_limit_bytes=24 * 2**20
        ),
    )(dest_map[None])

    blocks = pl.pallas_call(
        functools.partial(layer_kernel, count, cap),
        out_shape=(jax.ShapeDtypeStruct((cap, width), jnp.bfloat16),) * count,
        in_specs=[VMEM] * 7,
        out_specs=(pl.BlockSpec(memory_space=pl.ANY),) * count,
        scratch_shapes=[pltpu.VMEM((count, cap, width), jnp.bfloat16)]
        + [pltpu.VMEM((HEADS, run, LANES), jnp.bfloat16)] * 3
        + [pltpu.VMEM((run, width), jnp.bfloat16), pltpu.SemaphoreType.DMA((count,))],
        compiler_params=pltpu.CompilerParams(vmem_limit_bytes=56 * 2**20),
        cost_estimate=pl.CostEstimate(
            flops=16 * 10**9, bytes_accessed=12 * 10**6, transcendentals=8 * 10**6
        ),
    )(
        tokens, norm_gain, norm_bias, qkv_weight.T, out_weight, segment_ids[None], slot,
    )
    blocks = list(blocks)
    for shift in range(1, count):
        pairs = [(source, (source + shift) % count) for source in range(count)]
        blocks[shift] = lax.cond(
            needed[shift, 0] > 0,
            lambda rows, pairs=pairs: lax.ppermute(rows, "seq", pairs),
            lambda rows: rows,
            blocks[shift],
        )
    return pl.pallas_call(
        functools.partial(unpack_kernel, count, cap),
        out_shape=jax.ShapeDtypeStruct((run, width), jnp.bfloat16),
        in_specs=[VMEM]
        + [pl.BlockSpec(memory_space=pl.ANY)] * count,
        out_specs=VMEM,
        scratch_shapes=[
            pltpu.VMEM((run // cap, cap, width), jnp.bfloat16),
            pltpu.VMEM((run // cap, cap), jnp.int32),
            pltpu.VMEM((run, width), jnp.float32),
            pltpu.SemaphoreType.DMA((run // cap,)),
        ],
        compiler_params=pltpu.CompilerParams(vmem_limit_bytes=40 * 2**20),
    )(my_places, *blocks)


def solution(mesh):
    placed = (P(("dp", "seq"), None), P(), P(), P(), P(), P(("dp", "seq")), P(("dp", "seq")))
    return jax.shard_map(
        local, mesh=mesh, in_specs=placed, out_specs=P(("dp", "seq"), None), check_vma=False
    )
```
